32 devices in a mesh: parts: 2 (over x), param: 16 (over z, y, core).
Axes of the slice: x: 2, y: 2, z: 4, core: 2. Of those that a mesh axis runs over, the one named last changes fastest.
Arguments:
- inputs: bfloat16 [8192, 4096], P(('parts', 'param')), parts along dimension 0, may hold values from -7 to 7
- out_grads: bfloat16 [8192, 14336], P(('parts', 'param')), parts along dimension 0, may hold values from -7 to 7
- lengths: int32 [32], P(('parts', 'param')), parts along dimension 0, may hold values from 128 to 256, as said below
- example_ids: int32 [32], P(('parts', 'param')), parts along dimension 0, may hold values from 0 to 15, each once
- proj_seeds: int32 [4], P('parts'), parts along dimension 0, may hold values from 1 to 29999
Outputs:
- fisher: float32 [16384, 8192], P(('parts', 'param')), parts along dimension 0
- precond: float32 [32, 8192], P(('parts', 'param')), parts along dimension 0
- kernel: float32 [32, 16], P(('parts', 'param')), parts along dimension 0
The draws below stay inside these ranges and needn't reach their ends.
There are 2 independent parts, one for each index of `parts`. The reference program is written for one: setup_inputs(seed, part) draws one part's arguments, and reference() takes and returns one part's arrays. A program takes and returns all parts, laid end to end along the dimension named above; each array names one. Nothing has to cross between parts.
Inputs may be any that keep to these rules, and one draw needn't show every extreme that they name: `lengths`: each length is a multiple of 128; some example has the full 256 tokens and some has only 128. `example_ids`: a permutation of the group's example indices.
All inputs are finite; a program needn't handle non-finite values.
Results may differ from the reference program's by a relative error of at most 0.007.
The reference program's roundings to bfloat16 on the way (of `table_in`, `table_out`, `proj_in`, `proj_out`, `gradients` and `precond_low`) count: a program that leaves them out, or rounds other values in their place, can miss the bound.
Values may be sent and summed in bfloat16 or wider, within the bound.
A program may use at most 64 MiB of HBM per device.

```python
import math
import jax
import jax.numpy as jnp
from jax import lax

D = 4096
FF = 14336
K_IN = 64
K_OUT = 128
SLOT = 256
GRAIN = 128
EXAMPLES = 16
TOKENS = 4096


term_count = 4


def noise_level():
    mean_len = 0.5 * (SLOT + GRAIN)
    ratio = 2.0 * K_IN * K_OUT / EXAMPLES
    return math.sqrt(math.sqrt(1.0 + mean_len / ratio) - 1.0)


def token_factors(key, salt_value):
    tok_scale = jax.random.normal(jax.random.fold_in(key, 41), (TOKENS, 1), jnp.float32)
    weights = jax.random.normal(jax.random.fold_in(key, salt_value), (EXAMPLES, term_count), jnp.float32)
    return tok_scale * jnp.repeat(weights, SLOT, axis=0)


def token_field(key, salt_value, col_count):
    factors = token_factors(key, salt_value + 3)
    directions = jax.random.normal(jax.random.fold_in(key, salt_value + 4), (term_count, col_count), jnp.float32)
    shared = factors[:, 0:1] * directions[0:1, :]
    for term in range(1, term_count):
        shared = shared + factors[:, term:term + 1] * directions[term:term + 1, :]
    shared = shared * 0.5
    sigma = noise_level()
    noise_base = jax.random.normal(jax.random.fold_in(key, salt_value), (TOKENS, col_count), jnp.float32)
    return jnp.clip(shared + sigma * noise_base, -6.5, 6.5).astype(jnp.bfloat16)


def draw_inputs(key, part):
    return token_field(key, 11, D)


def draw_out_grads(key, part):
    return token_field(key, 31, FF)


def draw_lengths(key, part):
    step_count = SLOT // GRAIN
    levels = jax.random.randint(jax.random.fold_in(key, 21), (EXAMPLES,), 1, step_count + 1)
    longest = jax.random.randint(jax.random.fold_in(key, 22), (), 0, EXAMPLES)
    offset = jax.random.randint(jax.random.fold_in(key, 23), (), 1, EXAMPLES)
    shortest = (longest + offset) % EXAMPLES
    slot_index = jnp.arange(EXAMPLES, dtype=jnp.int32)
    levels = jnp.where(slot_index == longest, step_count, levels)
    levels = jnp.where(slot_index == shortest, 1, levels)
    return (levels * GRAIN).astype(jnp.int32)


def setup_inputs(seed: int = 0, part: int = 0) -> dict:
    key_list = jax.random.split(jax.random.key(seed), 6)
    part_keys = jax.random.split(jax.random.fold_in(key_list[5], part), 6)
    return {
        "inputs": draw_inputs(jax.random.fold_in(jax.random.fold_in(key_list[5], part), 71), part),
        "out_grads": draw_out_grads(jax.random.fold_in(jax.random.fold_in(key_list[5], part), 71), part),
        "lengths": draw_lengths(jax.random.fold_in(jax.random.fold_in(key_list[5], part), 71), part),
        "example_ids": jax.random.permutation(part_keys[3], EXAMPLES).astype(jnp.int32),
        "proj_seeds": jax.random.randint(part_keys[4], (2,), 1, 30000).astype(jnp.int32),
    }


damp_ratio = 0.5

def projection_table(out_dim, fan_in, seed_value):
    row_index = lax.broadcasted_iota(jnp.int32, (fan_in, out_dim), 1)
    col_index = lax.broadcasted_iota(jnp.int32, (fan_in, out_dim), 0)
    hashed = (row_index * 7919 + col_index * 3571 + seed_value * 9973) % 65521
    hashed = hashed * (hashed % 509 + 17) % 65521
    hashed = (hashed * 97 + row_index * 31 + col_index) % 65521
    uniform = hashed.astype(jnp.float32) * (2.0 / 65520.0) - 1.0
    return (uniform * math.sqrt(3.0 / fan_in)).astype(jnp.bfloat16)

def reference(inputs, out_grads, lengths, example_ids, proj_seeds):
    highest = lax.Precision.HIGHEST
    table_in = projection_table(K_IN, D, proj_seeds[0])
    table_out = projection_table(K_OUT, FF, proj_seeds[1])
    proj_in = jnp.dot(inputs.astype(jnp.float32), table_in.astype(jnp.float32), preferred_element_type=jnp.float32).astype(jnp.bfloat16)
    proj_out = jnp.dot(out_grads.astype(jnp.float32), table_out.astype(jnp.float32), preferred_element_type=jnp.float32).astype(jnp.bfloat16)
    live_rows = (lax.broadcasted_iota(jnp.int32, (EXAMPLES, SLOT), 1) < lengths[:, None]).reshape(EXAMPLES * SLOT, 1)
    proj_in = jnp.where(live_rows, proj_in, jnp.zeros_like(proj_in))
    outer = jnp.einsum('esi,eso->eio', proj_in.reshape(EXAMPLES, SLOT, K_IN).astype(jnp.float32), proj_out.reshape(EXAMPLES, SLOT, K_OUT).astype(jnp.float32), precision=highest)
    gradients = (outer * (1.0 / math.sqrt(SLOT))).reshape(EXAMPLES, K_IN * K_OUT).astype(jnp.bfloat16)
    wide = gradients.astype(jnp.float32)
    proj_width = K_IN * K_OUT
    fisher = jnp.dot(wide.T, wide, precision=highest) / EXAMPLES
    damping = damp_ratio * jnp.sum(wide * wide) / (EXAMPLES * proj_width)
    gram_matrix = jnp.dot(wide, wide.T, precision=highest)
    system = gram_matrix + damping * EXAMPLES * jnp.eye(EXAMPLES, dtype=jnp.float32)
    factor = jnp.linalg.cholesky(system)
    solved = jax.scipy.linalg.cho_solve((factor, True), gram_matrix)
    precond = (wide - jnp.dot(solved.T, wide, precision=highest)) / damping
    precond_low = precond.astype(jnp.bfloat16)
    by_slot = jnp.dot(wide, precond_low.astype(jnp.float32).T, precision=highest) / proj_width
    kernel = jnp.zeros((EXAMPLES, EXAMPLES), jnp.float32).at[example_ids[:, None], example_ids[None, :]].set(by_slot)
    return (fisher, precond, kernel)
```

```python
import functools
import math

import jax
import jax.numpy as jnp
from jax import lax
from jax.experimental import pallas as pl
from jax.experimental.pallas import tpu as pltpu
from jax.sharding import PartitionSpec as P

K_IN = 64
K_OUT = 128
PRIME = 65521
HALF = 32760
INV = pow(3571, -1, PRIME)
STEP_R = 7919 * INV % PRIME
STEP_S = 9973 * INV % PRIME
LANES = 128
HASH_ROWS = 640
CHUNK = 1024
damp_ratio = 0.5
MESH = pl.DeviceIdType.MESH


def fold(x):
    return (x & 65535) + (x >> 16) * 15


def wrap(x):
    return jnp.where(x >= PRIME, x - PRIME, x)


def hash_row(rows):
    g = lax.broadcasted_iota(jnp.int32, (rows, LANES), 0) * LANES + lax.broadcasted_iota(
        jnp.int32, (rows, LANES), 1
    )
    g = wrap(g)
    h1 = wrap(fold(g * 3571))
    m = h1 - ((h1 * 8241) >> 22) * 509
    m = jnp.where(m < 0, m + 509, m)
    h2 = fold(h1 * (m + 17))
    return wrap(fold(h2 * 97 + g)).astype(jnp.float32)


def make_table(hash_ref, table_ref, seed, count, fan_in):
    depth = fan_in // LANES
    scale = math.sqrt(3.0 / fan_in) / HALF
    lane = lax.broadcasted_iota(jnp.int32, (depth, LANES), 1)
    start = lax.rem(seed * STEP_S, PRIME)

    def body(r, offset):
        row = offset >> 7
        shift = offset & 127
        c = 31 * r - offset
        c = jnp.where(c < 0, c + PRIME, c)
        add = (c - HALF).astype(jnp.float32)
        x = jnp.where(
            lane >= shift, hash_ref[pl.ds(row, depth), :], hash_ref[pl.ds(row + 1, depth), :]
        )
        y = x + add
        y = jnp.where(y > HALF, y - PRIME, y) * scale
        table_ref[pl.ds(r, depth, stride=count), :] = pltpu.roll(y, (128 - shift) & 127, 1)
        offset = offset + STEP_R
        return jnp.where(offset >= PRIME, offset - PRIME, offset)

    lax.fori_loop(0, count, body, start, unroll=4)


def table_block(table_ref, count, first, blocks):
    return jnp.concatenate(
        [
            table_ref[(first + b) * count : (first + b + 1) * count, :].astype(jnp.bfloat16)
            for b in range(blocks)
        ],
        axis=1,
    )


def nt_dot(a, b):
    return lax.dot_general(a, b, (((1,), (1,)), ((), ())), preferred_element_type=jnp.float32)


def project_kernel(
    seeds, lengths, in_hbm, og_hbm, grad_ref, hash_ref, tin, tout, inbuf, ogbuf, in_sem, og_sem
):
    tokens, d_in = in_hbm.shape
    d_out = og_hbm.shape[1]
    chunks = d_out // CHUNK
    in_copy = pltpu.make_async_copy(in_hbm, inbuf, in_sem)
    in_copy.start()
    copies = []
    for c in range(chunks):
        cols = pl.ds(c * CHUNK, CHUNK)
        copy = pltpu.make_async_copy(og_hbm.at[:, cols], ogbuf.at[:, cols], og_sem.at[c])
        copy.start()
        copies.append(copy)
    hash_ref[...] = hash_row(HASH_ROWS)
    make_table(hash_ref, tin, seeds[0], K_IN, d_in)
    make_table(hash_ref, tout, seeds[1], K_OUT, d_out)
    in_copy.wait()
    per = CHUNK // LANES
    proj_in = jnp.zeros((K_IN, tokens), jnp.float32)
    for c in range(d_in // CHUNK):
        proj_in += nt_dot(
            table_block(tin, K_IN, c * per, per), inbuf[:, c * CHUNK : (c + 1) * CHUNK]
        )
    proj_out = jnp.zeros((K_OUT, tokens), jnp.float32)
    for c in range(chunks):
        copies[c].wait()
        proj_out += nt_dot(
            table_block(tout, K_OUT, c * per, per), ogbuf[:, c * CHUNK : (c + 1) * CHUNK]
        )
    live = lax.broadcasted_iota(jnp.int32, (K_IN, tokens), 1) < lengths[0]
    proj_in = jnp.where(live, proj_in, 0.0).astype(jnp.bfloat16)
    outer = nt_dot(proj_in, proj_out.astype(jnp.bfloat16))
    grad_ref[...] = (outer * (1.0 / math.sqrt(tokens))).astype(jnp.bfloat16)


def gather_kernel(n, ids, grad, gat, gid, send, recv, id_send, id_recv):
    me = lax.axis_index("param")
    chips = n // 2
    chip, core = me // 2, lax.rem(me, 2)
    sibling = chip * 2 + 1 - core
    peers = [lax.rem(chip + off, chips) * 2 + core for off in range(1, chips)]

    barrier = pltpu.get_barrier_semaphore()
    for peer in [sibling] + peers:
        pl.semaphore_signal(barrier, inc=1, device_id={"param": peer}, device_id_type=MESH)
    gat[me] = grad[...]
    gid[me] = jnp.zeros((1, LANES), jnp.int32) + ids[0]
    pl.semaphore_wait(barrier, chips)

    def push(block, target, slot):
        out = []
        for ref, s, r in ((gid, id_send, id_recv), (gat, send, recv)):
            copy = pltpu.make_async_remote_copy(
                src_ref=ref.at[block],
                dst_ref=ref.at[block],
                send_sem=s.at[slot],
                recv_sem=r.at[block],
                device_id={"param": target},
                device_id_type=MESH,
            )
            copy.start()
            out.append(copy)
        return out

    def arrived(block):
        for ref, s, r in ((gid, id_send, id_recv), (gat, send, recv)):
            pltpu.make_async_remote_copy(
                src_ref=ref.at[block],
                dst_ref=ref.at[block],
                send_sem=s.at[0],
                recv_sem=r.at[block],
                device_id={"param": sibling},
                device_id_type=MESH,
            ).wait_recv()

    started = []
    for off, peer in enumerate(peers):
        started += push(me, peer, off)
    started += push(me, sibling, chips - 1)
    for off in range(1, chips):
        block = lax.rem(chip - off + chips, chips) * 2 + core
        arrived(block)
        started += push(block, sibling, chips - 1 + off)
    for off in range(chips):
        arrived(lax.rem(chip - off + chips, chips) * 2 + 1 - core)
    for copy in started:
        copy.wait_send()


def finish_kernel(n, gat, gid, fisher, precond, kernel, wide, low, rows, prec, fbuf, sem):
    me = lax.axis_index("param")
    width = K_IN * K_OUT
    block = width // n
    wide[...] = gat[...].astype(jnp.float32).reshape(n * K_IN, K_OUT)
    for i in range(K_IN):
        low[:, i * K_OUT : (i + 1) * K_OUT] = wide[pl.ds(i, n, stride=K_IN), :].astype(jnp.bfloat16)
    first = me * block
    for i in range(max(1, block // K_OUT)):
        part = wide[pl.ds(first // K_OUT + i, n, stride=K_IN), :] * (1.0 / n)
        if block < K_OUT:
            part = pltpu.roll(part, lax.rem(K_OUT - lax.rem(first, K_OUT), K_OUT), 1)
        rows[i * K_OUT : (i + 1) * K_OUT, :] = part.T.astype(jnp.bfloat16)
    columns = rows[0:block, :]
    copies = []
    for c in range(width // CHUNK):
        cols = pl.ds(c * CHUNK, CHUNK)
        fbuf[:, cols] = jnp.dot(columns, low[:, cols], preferred_element_type=jnp.float32)
        copy = pltpu.make_async_copy(fbuf.at[:, cols], fisher.at[:, cols], sem.at[c])
        copy.start()
        copies.append(copy)

    gram = jnp.zeros((n, n), jnp.float32)
    for c in range(width // CHUNK):
        cols = pl.ds(c * CHUNK, CHUNK)
        gram += nt_dot(low[:, cols], low[:, cols])
    sub = lax.broadcasted_iota(jnp.int32, (n, n), 0)
    lane = lax.broadcasted_iota(jnp.int32, (n, n), 1)
    eye = sub == lane
    square_sum = jnp.sum(jnp.where(eye, gram, 0.0), keepdims=True)
    damping = damp_ratio * square_sum / (n * width)
    system = gram + jnp.where(eye, damping * n, 0.0)

    def sweep(k, m):
        col = jnp.sum(jnp.where(lane == k, m, 0.0), axis=1, keepdims=True)
        row = jnp.sum(jnp.where(sub == k, m, 0.0), axis=0, keepdims=True)
        pivot = 1.0 / jnp.sum(jnp.where(eye & (sub == k), m, 0.0), keepdims=True)
        scaled = row * pivot
        out = m - col * scaled
        out = jnp.where(sub == k, scaled, out)
        out = jnp.where(lane == k, col * pivot, out)
        return jnp.where(eye & (sub == k), -pivot, out)

    if n <= 16:
        for k in range(n):
            system = sweep(k, system)
    else:
        system = lax.fori_loop(0, n, sweep, system)
    inverse = system * (-float(n))
    high = inverse.astype(jnp.bfloat16)
    rest = inverse - high.astype(jnp.float32)
    mid = rest.astype(jnp.bfloat16)
    last = (rest - mid.astype(jnp.float32)).astype(jnp.bfloat16)
    pair = jnp.zeros((n, n), jnp.float32)
    for c in range(width // CHUNK):
        cols = pl.ds(c * CHUNK, CHUNK)
        g = low[:, cols]
        p = jnp.dot(last, g, preferred_element_type=jnp.float32)
        p += jnp.dot(mid, g, preferred_element_type=jnp.float32)
        p += jnp.dot(high, g, preferred_element_type=jnp.float32)
        prec[:, cols] = p
        pair += nt_dot(p.astype(jnp.bfloat16), g)
    precond[...] = prec[pl.ds(me, 1), :]
    ids = gid[:, 0, :][:, 0:n]
    own = jnp.sum(jnp.where(eye & (ids == me), 1.0, 0.0), axis=0, keepdims=True)
    by_slot = jnp.sum(pair * own, axis=1, keepdims=True)
    kernel[...] = jnp.sum(jnp.where(ids == lane, by_slot, 0.0), axis=0, keepdims=True) * (
        1.0 / width
    )
    for copy in copies:
        copy.wait()


def vmem(shape, dtype=jnp.float32):
    return pltpu.VMEM(shape, dtype)


def local(n, inputs, out_grads, lengths, example_ids, proj_seeds):
    any_space = pl.BlockSpec(memory_space=pl.ANY)
    smem = pl.BlockSpec(memory_space=pltpu.SMEM)
    vm = pl.BlockSpec(memory_space=pltpu.VMEM)
    tokens, d_in = inputs.shape
    d_out = out_grads.shape[1]
    width = K_IN * K_OUT
    grads = pl.pallas_call(
        project_kernel,
        out_shape=jax.ShapeDtypeStruct((K_IN, K_OUT), jnp.bfloat16),
        in_specs=[smem, smem, any_space, any_space],
        out_specs=vm,
        scratch_shapes=[
            vmem((HASH_ROWS, LANES)),
            vmem((d_in // LANES * K_IN, LANES)),
            vmem((d_out // LANES * K_OUT, LANES)),
            vmem((tokens, d_in), jnp.bfloat16),
            vmem((tokens, d_out), jnp.bfloat16),
            pltpu.SemaphoreType.DMA,
            pltpu.SemaphoreType.DMA((d_out // CHUNK,)),
        ],
        compiler_params=pltpu.CompilerParams(vmem_limit_bytes=56 << 20),
    )(proj_seeds, lengths, inputs, out_grads)
    gat, gid = pl.pallas_call(
        functools.partial(gather_kernel, n),
        out_shape=(
            jax.ShapeDtypeStruct((n, K_IN, K_OUT), jnp.bfloat16),
            jax.ShapeDtypeStruct((n, 1, LANES), jnp.int32),
        ),
        in_specs=[smem, vm],
        out_specs=(vm, vm),
        scratch_shapes=[
            pltpu.SemaphoreType.DMA((n,)),
            pltpu.SemaphoreType.DMA((n,)),
            pltpu.SemaphoreType.DMA((n,)),
            pltpu.SemaphoreType.DMA((n,)),
        ],
        compiler_params=pltpu.CompilerParams(collective_id=0, has_side_effects=True),
    )(example_ids, grads)
    return pl.pallas_call(
        functools.partial(finish_kernel, n),
        out_shape=(
            jax.ShapeDtypeStruct((width // n, width), jnp.float32),
            jax.ShapeDtypeStruct((1, width), jnp.float32),
            jax.ShapeDtypeStruct((1, n), jnp.float32),
        ),
        in_specs=[vm, vm],
        out_specs=(any_space, vm, vm),
        scratch_shapes=[
            vmem((n * K_IN, K_OUT)),
            vmem((n, width), jnp.bfloat16),
            vmem((max(width // n, K_OUT), n), jnp.bfloat16),
            vmem((n, width)),
            vmem((width // n, width)),
            pltpu.SemaphoreType.DMA((width // CHUNK,)),
        ],
        compiler_params=pltpu.CompilerParams(vmem_limit_bytes=48 << 20),
    )(gat, gid)


def solution(mesh):
    rows = P(("parts", "param"), None)
    flat = P(("parts", "param"))
    return jax.shard_map(
        functools.partial(local, mesh.shape["param"]),
        mesh=mesh,
        in_specs=(rows, rows, flat, flat, P("parts")),
        out_specs=(rows, rows, rows),
        check_vma=False,
    )
```

```python
import functools
import math

import jax
import jax.numpy as jnp
from jax import lax
from jax.experimental import pallas as pl
from jax.experimental.pallas import tpu as pltpu
from jax.sharding import PartitionSpec as P

K_IN = 64
K_OUT = 128
PRIME = 65521
HALF = 32760
INV = pow(3571, -1, PRIME)
STEP_R = 7919 * INV % PRIME
STEP_S = 9973 * INV % PRIME
LANES = 128
HASH_ROWS = 640
CHUNK = 1024
PAD = 8
damp_ratio = 0.5
MESH = pl.DeviceIdType.MESH


def fold(x):
    return (x & 65535) + (x >> 16) * 15


def wrap(x):
    return jnp.where(x >= PRIME, x - PRIME, x)


def hash_row(rows):
    g = lax.broadcasted_iota(jnp.int32, (rows, LANES), 0) * LANES + lax.broadcasted_iota(
        jnp.int32, (rows, LANES), 1
    )
    g = wrap(g)
    h1 = wrap(fold(g * 3571))
    m = h1 - ((h1 * 8241) >> 22) * 509
    m = jnp.where(m < 0, m + 509, m)
    h2 = fold(h1 * (m + 17))
    return wrap(fold(h2 * 97 + g)).astype(jnp.float32)


def make_table(hash_ref, table_ref, seed, count, fan_in):
    depth = fan_in // LANES
    scale = math.sqrt(3.0 / fan_in) / HALF
    lane = lax.broadcasted_iota(jnp.int32, (depth, LANES), 1)
    start = lax.rem(seed * STEP_S, PRIME)

    def body(r, offset):
        row = offset >> 7
        shift = offset & 127
        c = 31 * r - offset
        c = jnp.where(c < 0, c + PRIME, c)
        add = (c - HALF).astype(jnp.float32)
        x = jnp.where(
            lane >= shift, hash_ref[pl.ds(row, depth), :], hash_ref[pl.ds(row + 1, depth), :]
        )
        y = x + add
        y = jnp.where(y > HALF, y - PRIME, y) * scale
        table_ref[pl.ds(r, depth, stride=count + PAD), :] = pltpu.roll(y, (128 - shift) & 127, 1)
        offset = offset + STEP_R
        return jnp.where(offset >= PRIME, offset - PRIME, offset)

    lax.fori_loop(0, count, body, start, unroll=8)


def table_block(table_ref, count, first, blocks):
    return jnp.concatenate(
        [
            table_ref[(first + b) * (count + PAD) : (first + b) * (count + PAD) + count, :].astype(
                jnp.bfloat16
            )
            for b in range(blocks)
        ],
        axis=1,
    )


def nt_dot(a, b):
    return lax.dot_general(a, b, (((1,), (1,)), ((), ())), preferred_element_type=jnp.float32)


def project_gather_kernel(
    n,
    seeds,
    lengths,
    ids,
    in_hbm,
    og_hbm,
    gat,
    gid,
    hash_ref,
    tin,
    tout,
    inbuf,
    ogbuf,
    in_sem,
    og_sem,
    send,
    recv,
    id_send,
    id_recv,
):
    me = lax.axis_index("param")
    chips = n // 2
    chip, core = me // 2, lax.rem(me, 2)
    sibling = chip * 2 + 1 - core
    peers = [lax.rem(chip + off, chips) * 2 + core for off in range(1, chips)]
    grad_lane, id_lane = (gat, send, recv), (gid, id_send, id_recv)

    barrier = pltpu.get_barrier_semaphore()
    for peer in [sibling] + peers:
        pl.semaphore_signal(barrier, inc=1, device_id={"param": peer}, device_id_type=MESH)

    def push(lane, block, target, slot):
        ref, s, r = lane
        copy = pltpu.make_async_remote_copy(
            src_ref=ref.at[block],
            dst_ref=ref.at[block],
            send_sem=s.at[slot],
            recv_sem=r.at[block],
            device_id={"param": target},
            device_id_type=MESH,
        )
        copy.start()
        return copy

    def arrived(lane, block):
        ref, s, r = lane
        pltpu.make_async_remote_copy(
            src_ref=ref.at[block],
            dst_ref=ref.at[block],
            send_sem=s.at[0],
            recv_sem=r.at[block],
            device_id={"param": sibling},
            device_id_type=MESH,
        ).wait_recv()

    def send_own(lane):
        out = [push(lane, me, peer, off) for off, peer in enumerate(peers)]
        return out + [push(lane, me, sibling, chips - 1)]

    def forward(lane):
        out = []
        for off in range(1, chips):
            block = lax.rem(chip - off + chips, chips) * 2 + core
            arrived(lane, block)
            out.append(push(lane, block, sibling, chips - 1 + off))
        return out

    def collect(lane):
        for off in range(chips):
            arrived(lane, lax.rem(chip - off + chips, chips) * 2 + 1 - core)

    tokens, d_in = in_hbm.shape
    d_out = og_hbm.shape[1]
    in_copy = pltpu.make_async_copy(in_hbm, inbuf, in_sem)
    in_copy.start()
    og_copy = pltpu.make_async_copy(og_hbm, ogbuf, og_sem)
    og_copy.start()
    gid[me] = jnp.zeros((1, LANES), jnp.int32) + ids[0]
    hash_ref[...] = hash_row(HASH_ROWS)
    make_table(hash_ref, tin, seeds[0], K_IN, d_in)
    pl.semaphore_wait(barrier, chips)
    started = send_own(id_lane)
    make_table(hash_ref, tout, seeds[1], K_OUT, d_out)
    started += forward(id_lane)
    per = CHUNK // LANES
    in_copy.wait()
    proj_in = jnp.zeros((tokens, K_IN), jnp.float32)
    for c in range(d_in // CHUNK):
        proj_in += nt_dot(
            inbuf[:, c * CHUNK : (c + 1) * CHUNK], table_block(tin, K_IN, c * per, per)
        )
    og_copy.wait()
    proj_out = jnp.zeros((tokens, K_OUT), jnp.float32)
    for c in range(d_out // CHUNK):
        proj_out += nt_dot(
            ogbuf[:, c * CHUNK : (c + 1) * CHUNK], table_block(tout, K_OUT, c * per, per)
        )
    live = lax.broadcasted_iota(jnp.int32, (tokens, K_IN), 0) < lengths[0]
    proj_in = jnp.where(live, proj_in, 0.0).T.astype(jnp.bfloat16)
    outer = jnp.dot(proj_in, proj_out.astype(jnp.bfloat16), preferred_element_type=jnp.float32)
    gat[me] = (outer * (1.0 / math.sqrt(tokens))).astype(jnp.bfloat16)
    started += send_own(grad_lane)
    collect(id_lane)
    started += forward(grad_lane)
    collect(grad_lane)
    for copy in started:
        copy.wait_send()


def finish_kernel(
    n, gat_any, gid_any, fisher, precond, kernel, gat, gid, wide, low, rows, prec, fbuf, sem, arg_sem
):
    gat_copy = pltpu.make_async_copy(gat_any, gat, arg_sem.at[0])
    gat_copy.start()
    gid_copy = pltpu.make_async_copy(gid_any, gid, arg_sem.at[1])
    gid_copy.start()
    me = lax.axis_index("param")
    width = K_IN * K_OUT
    block = width // n
    gat_copy.wait()
    wide[...] = gat[...].astype(jnp.float32).reshape(n * K_IN, K_OUT)
    for i in range(K_IN):
        low[:, i * K_OUT : (i + 1) * K_OUT] = wide[pl.ds(i, n, stride=K_IN), :].astype(jnp.bfloat16)
    first = me * block
    for i in range(max(1, block // K_OUT)):
        part = wide[pl.ds(first // K_OUT + i, n, stride=K_IN), :] * (1.0 / n)
        if block < K_OUT:
            part = pltpu.roll(part, lax.rem(K_OUT - lax.rem(first, K_OUT), K_OUT), 1)
        rows[i * K_OUT : (i + 1) * K_OUT, :] = part.T.astype(jnp.bfloat16)
    columns = rows[0:block, :]
    copies = []
    for c in range(width // CHUNK):
        cols = pl.ds(c * CHUNK, CHUNK)
        fbuf[:, cols] = jnp.dot(columns, low[:, cols], preferred_element_type=jnp.float32)
        copy = pltpu.make_async_copy(fbuf.at[:, cols], fisher.at[:, cols], sem.at[c])
        copy.start()
        copies.append(copy)

    gram = jnp.zeros((n, n), jnp.float32)
    for c in range(width // CHUNK):
        cols = pl.ds(c * CHUNK, CHUNK)
        gram += nt_dot(low[:, cols], low[:, cols])
    sub = lax.broadcasted_iota(jnp.int32, (n, n), 0)
    lane = lax.broadcasted_iota(jnp.int32, (n, n), 1)
    eye = sub == lane
    square_sum = jnp.sum(jnp.where(eye, gram, 0.0), keepdims=True)
    damping = damp_ratio * square_sum / (n * width)
    system = gram + jnp.where(eye, damping * n, 0.0)

    def sweep(k, m):
        col = jnp.sum(jnp.where(lane == k, m, 0.0), axis=1, keepdims=True)
        row = jnp.sum(jnp.where(sub == k, m, 0.0), axis=0, keepdims=True)
        pivot = 1.0 / jnp.sum(jnp.where(eye & (sub == k), m, 0.0), keepdims=True)
        scaled = row * pivot
        out = m - col * scaled
        out = jnp.where(sub == k, scaled, out)
        out = jnp.where(lane == k, col * pivot, out)
        return jnp.where(eye & (sub == k), -pivot, out)

    if n <= 16:
        for k in range(n):
            system = sweep(k, system)
    else:
        system = lax.fori_loop(0, n, sweep, system)
    inverse = system * (-float(n))
    high = inverse.astype(jnp.bfloat16)
    rest = inverse - high.astype(jnp.float32)
    mid = rest.astype(jnp.bfloat16)
    last = (rest - mid.astype(jnp.float32)).astype(jnp.bfloat16)
    pair = jnp.zeros((n, n), jnp.float32)
    for c in range(width // CHUNK):
        cols = pl.ds(c * CHUNK, CHUNK)
        g = low[:, cols]
        p = jnp.dot(last, g, preferred_element_type=jnp.float32)
        p += jnp.dot(mid, g, preferred_element_type=jnp.float32)
        p += jnp.dot(high, g, preferred_element_type=jnp.float32)
        prec[:, cols] = p
        pair += nt_dot(p.astype(jnp.bfloat16), g)
    precond[...] = prec[pl.ds(me, 1), :]
    gid_copy.wait()
    ids = gid[:, 0, :][:, 0:n]
    own = jnp.sum(jnp.where(eye & (ids == me), 1.0, 0.0), axis=0, keepdims=True)
    by_slot = jnp.sum(pair * own, axis=1, keepdims=True)
    kernel[...] = jnp.sum(jnp.where(ids == lane, by_slot, 0.0), axis=0, keepdims=True) * (
        1.0 / width
    )
    for copy in copies:
        copy.wait()


def vmem(shape, dtype=jnp.float32):
    return pltpu.VMEM(shape, dtype)


def local(n, inputs, out_grads, lengths, example_ids, proj_seeds):
    any_space = pl.BlockSpec(memory_space=pl.ANY)
    smem = pl.BlockSpec(memory_space=pltpu.SMEM)
    vm = pl.BlockSpec(memory_space=pltpu.VMEM)
    tokens, d_in = inputs.shape
    d_out = out_grads.shape[1]
    width = K_IN * K_OUT
    gat, gid = pl.pallas_call(
        functools.partial(project_gather_kernel, n),
        out_shape=(
            jax.ShapeDtypeStruct((n, K_IN, K_OUT), jnp.bfloat16),
            jax.ShapeDtypeStruct((n, 1, LANES), jnp.int32),
        ),
        in_specs=[smem, smem, smem, any_space, any_space],
        out_specs=(vm, vm),
        scratch_shapes=[
            vmem((HASH_ROWS, LANES)),
            vmem((d_in // LANES * (K_IN + PAD), LANES)),
            vmem((d_out // LANES * (K_OUT + PAD), LANES)),
            vmem((tokens, d_in), jnp.bfloat16),
            vmem((tokens, d_out), jnp.bfloat16),
            pltpu.SemaphoreType.DMA,
            pltpu.SemaphoreType.DMA,
            pltpu.SemaphoreType.DMA((n,)),
            pltpu.SemaphoreType.DMA((n,)),
            pltpu.SemaphoreType.DMA((n,)),
            pltpu.SemaphoreType.DMA((n,)),
        ],
        compiler_params=pltpu.CompilerParams(
            collective_id=0, has_side_effects=True, vmem_limit_bytes=60 << 20
        ),
    )(proj_seeds, lengths, example_ids, inputs, out_grads)
    return pl.pallas_call(
        functools.partial(finish_kernel, n),
        out_shape=(
            jax.ShapeDtypeStruct((width // n, width), jnp.float32),
            jax.ShapeDtypeStruct((1, width), jnp.float32),
            jax.ShapeDtypeStruct((1, n), jnp.float32),
        ),
        in_specs=[any_space, any_space],
        out_specs=(any_space, vm, vm),
        scratch_shapes=[
            vmem((n, K_IN, K_OUT), jnp.bfloat16),
            vmem((n, 1, LANES), jnp.int32),
            vmem((n * K_IN, K_OUT)),
            vmem((n, width), jnp.bfloat16),
            vmem((max(width // n, K_OUT), n), jnp.bfloat16),
            vmem((n, width)),
            vmem((width // n, width)),
            pltpu.SemaphoreType.DMA((width // CHUNK,)),
            pltpu.SemaphoreType.DMA((2,)),
        ],
        compiler_params=pltpu.CompilerParams(vmem_limit_bytes=60 << 20),
    )(gat, gid)


def solution(mesh):
    rows = P(("parts", "param"), None)
    flat = P(("parts", "param"))
    return jax.shard_map(
        functools.partial(local, mesh.shape["param"]),
        mesh=mesh,
        in_specs=(rows, rows, flat, flat, P("parts")),
        out_specs=(rows, rows, rows),
        check_vma=False,
    )
```

```python
import functools
import math

import jax
import jax.numpy as jnp
from jax import lax
from jax.experimental import pallas as pl
from jax.experimental.pallas import tpu as pltpu
from jax.sharding import PartitionSpec as P

K_IN = 64
K_OUT = 128
PRIME = 65521
HALF = 32760
INV = pow(3571, -1, PRIME)
STEP_R = 7919 * INV % PRIME
STEP_S = 9973 * INV % PRIME
LANES = 128
HASH_ROWS = 640
CHUNK = 1024
PAD = 8
damp_ratio = 0.5
MESH = pl.DeviceIdType.MESH


def fold(x):
    return (x & 65535) + (x >> 16) * 15


def wrap(x):
    return jnp.where(x >= PRIME, x - PRIME, x)


def hash_row(rows):
    g = lax.broadcasted_iota(jnp.int32, (rows, LANES), 0) * LANES + lax.broadcasted_iota(
        jnp.int32, (rows, LANES), 1
    )
    g = wrap(g)
    h1 = wrap(fold(g * 3571))
    m = h1 - ((h1 * 8241) >> 22) * 509
    m = jnp.where(m < 0, m + 509, m)
    h2 = fold(h1 * (m + 17))
    return wrap(fold(h2 * 97 + g)).astype(jnp.float32)


def make_table(hash_ref, table_ref, seed, count, fan_in):
    depth = fan_in // LANES
    scale = math.sqrt(3.0 / fan_in) / HALF
    lane = lax.broadcasted_iota(jnp.int32, (depth, LANES), 1)
    start = lax.rem(seed * STEP_S, PRIME)

    def body(r, offset):
        row = offset >> 7
        shift = offset & 127
        c = 31 * r - offset
        c = jnp.where(c < 0, c + PRIME, c)
        add = (c - HALF).astype(jnp.float32)
        x = jnp.where(
            lane >= shift, hash_ref[pl.ds(row, depth), :], hash_ref[pl.ds(row + 1, depth), :]
        )
        y = x + add
        y = jnp.where(y > HALF, y - PRIME, y) * scale
        table_ref[pl.ds(r, depth, stride=count + PAD), :] = pltpu.roll(y, (128 - shift) & 127, 1)
        offset = offset + STEP_R
        return jnp.where(offset >= PRIME, offset - PRIME, offset)

    lax.fori_loop(0, count, body, start, unroll=8)


def table_block(table_ref, count, first, blocks):
    return jnp.concatenate(
        [
            table_ref[(first + b) * (count + PAD) : (first + b) * (count + PAD) + count, :].astype(
                jnp.bfloat16
            )
            for b in range(blocks)
        ],
        axis=1,
    )


def nt_dot(a, b):
    return lax.dot_general(a, b, (((1,), (1,)), ((), ())), preferred_element_type=jnp.float32)


def project_gather_kernel(
    n,
    seeds,
    lengths,
    ids,
    in_hbm,
    og_hbm,
    gat,
    gid,
    hash_ref,
    tin,
    tout,
    inbuf,
    ogbuf,
    in_sem,
    og_sem,
    send,
    recv,
    id_send,
    id_recv,
):
    me = lax.axis_index("param")
    peers = [lax.rem(me + off, n) for off in range(1, n)]
    grad_lane, id_lane = (gat, send, recv), (gid, id_send, id_recv)

    barrier = pltpu.get_barrier_semaphore()
    for peer in peers:
        pl.semaphore_signal(barrier, inc=1, device_id={"param": peer}, device_id_type=MESH)

    def push(lane, block, target, slot):
        ref, s, r = lane
        copy = pltpu.make_async_remote_copy(
            src_ref=ref.at[block],
            dst_ref=ref.at[block],
            send_sem=s.at[slot],
            recv_sem=r.at[block],
            device_id={"param": target},
            device_id_type=MESH,
        )
        copy.start()
        return copy

    def arrived(lane, block):
        ref, s, r = lane
        pltpu.make_async_remote_copy(
            src_ref=ref.at[block],
            dst_ref=ref.at[block],
            send_sem=s.at[0],
            recv_sem=r.at[block],
            device_id={"param": lax.rem(me + 1, n)},
            device_id_type=MESH,
        ).wait_recv()

    def send_own(lane):
        return [push(lane, me, peer, off) for off, peer in enumerate(peers)]

    def collect(lane):
        for off in range(1, n):
            arrived(lane, lax.rem(me + off, n))

    tokens, d_in = in_hbm.shape
    d_out = og_hbm.shape[1]
    in_copy = pltpu.make_async_copy(in_hbm, inbuf, in_sem)
    in_copy.start()
    og_copy = pltpu.make_async_copy(og_hbm, ogbuf, og_sem)
    og_copy.start()
    gid[me] = jnp.zeros((1, LANES), jnp.int32) + ids[0]
    hash_ref[...] = hash_row(HASH_ROWS)
    make_table(hash_ref, tin, seeds[0], K_IN, d_in)
    pl.semaphore_wait(barrier, n - 1)
    started = send_own(id_lane)
    make_table(hash_ref, tout, seeds[1], K_OUT, d_out)
    per = CHUNK // LANES
    in_copy.wait()
    proj_in = jnp.zeros((tokens, K_IN), jnp.float32)
    for c in range(d_in // CHUNK):
        proj_in += nt_dot(
            inbuf[:, c * CHUNK : (c + 1) * CHUNK], table_block(tin, K_IN, c * per, per)
        )
    og_copy.wait()
    proj_out = jnp.zeros((tokens, K_OUT), jnp.float32)
    for c in range(d_out // CHUNK):
        proj_out += nt_dot(
            ogbuf[:, c * CHUNK : (c + 1) * CHUNK], table_block(tout, K_OUT, c * per, per)
        )
    live = lax.broadcasted_iota(jnp.int32, (tokens, K_IN), 0) < lengths[0]
    proj_in = jnp.where(live, proj_in, 0.0).T.astype(jnp.bfloat16)
    outer = jnp.dot(proj_in, proj_out.astype(jnp.bfloat16), preferred_element_type=jnp.float32)
    gat[me] = (outer * (1.0 / math.sqrt(tokens))).astype(jnp.bfloat16)
    started += send_own(grad_lane)
    collect(id_lane)
    collect(grad_lane)
    for copy in started:
        copy.wait_send()


def finish_kernel(
    n, gat_any, gid_any, fisher, precond, kernel, gat, gid, wide, low, rows, prec, fbuf, sem, arg_sem
):
    gat_copy = pltpu.make_async_copy(gat_any, gat, arg_sem.at[0])
    gat_copy.start()
    gid_copy = pltpu.make_async_copy(gid_any, gid, arg_sem.at[1])
    gid_copy.start()
    me = lax.axis_index("param")
    width = K_IN * K_OUT
    block = width // n
    gat_copy.wait()
    wide[0 : n * K_IN, :] = gat[...].astype(jnp.float32).reshape(n * K_IN, K_OUT)
    for i in range(K_IN):
        low[:, i * K_OUT : (i + 1) * K_OUT] = wide[pl.ds(i, n, stride=K_IN), :].astype(jnp.bfloat16)
    first = me * block
    for i in range(max(1, block // K_OUT)):
        part = wide[pl.ds(first // K_OUT + i, n, stride=K_IN), :] * (1.0 / n)
        if block < K_OUT:
            part = pltpu.roll(part, lax.rem(K_OUT - lax.rem(first, K_OUT), K_OUT), 1)
        rows[i * K_OUT : (i + 1) * K_OUT, :] = part.T.astype(jnp.bfloat16)
    columns = rows[0:block, :]
    copies = []
    for c in range(width // CHUNK):
        cols = pl.ds(c * CHUNK, CHUNK)
        fbuf[:, cols] = jnp.dot(columns, low[:, cols], preferred_element_type=jnp.float32)
        copy = pltpu.make_async_copy(fbuf.at[:, cols], fisher.at[:, cols], sem.at[c])
        copy.start()
        copies.append(copy)

    gram = jnp.zeros((n, n), jnp.float32)
    for c in range(width // CHUNK):
        cols = pl.ds(c * CHUNK, CHUNK)
        gram += nt_dot(low[:, cols], low[:, cols])
    sub = lax.broadcasted_iota(jnp.int32, (n, n), 0)
    lane = lax.broadcasted_iota(jnp.int32, (n, n), 1)
    eye = sub == lane
    square_sum = jnp.sum(jnp.where(eye, gram, 0.0), keepdims=True)
    damping = damp_ratio * square_sum / (n * width)
    system = gram + jnp.where(eye, damping * n, 0.0)

    def sweep(k, m):
        col = jnp.sum(jnp.where(lane == k, m, 0.0), axis=1, keepdims=True)
        row = jnp.sum(jnp.where(sub == k, m, 0.0), axis=0, keepdims=True)
        pivot = 1.0 / jnp.sum(jnp.where(eye & (sub == k), m, 0.0), keepdims=True)
        scaled = row * pivot
        out = m - col * scaled
        out = jnp.where(sub == k, scaled, out)
        out = jnp.where(lane == k, col * pivot, out)
        return jnp.where(eye & (sub == k), -pivot, out)

    if n <= 16:
        for k in range(n):
            system = sweep(k, system)
    else:
        system = lax.fori_loop(0, n, sweep, system)
    inverse = system * (-float(n))
    high = inverse.astype(jnp.bfloat16)
    rest = inverse - high.astype(jnp.float32)
    mid = rest.astype(jnp.bfloat16)
    last = (rest - mid.astype(jnp.float32)).astype(jnp.bfloat16)
    pair = jnp.zeros((n, n), jnp.float32)
    for c in range(width // CHUNK):
        cols = pl.ds(c * CHUNK, CHUNK)
        g = low[:, cols]
        p = jnp.dot(last, g, preferred_element_type=jnp.float32)
        p += jnp.dot(mid, g, preferred_element_type=jnp.float32)
        p += jnp.dot(high, g, preferred_element_type=jnp.float32)
        prec[:, cols] = p
        pair += nt_dot(p.astype(jnp.bfloat16), g)
    precond[...] = prec[pl.ds(me, 1), :]
    gid_copy.wait()
    ids = gid[:, 0, :][:, 0:n]
    own = jnp.sum(jnp.where(eye & (ids == me), 1.0, 0.0), axis=0, keepdims=True)
    by_slot = jnp.sum(pair * own, axis=1, keepdims=True)
    kernel[...] = jnp.sum(jnp.where(ids == lane, by_slot, 0.0), axis=0, keepdims=True) * (
        1.0 / width
    )
    for copy in copies:
        copy.wait()


def vmem(shape, dtype=jnp.float32):
    return pltpu.VMEM(shape, dtype)


def local(n, inputs, out_grads, lengths, example_ids, proj_seeds):
    any_space = pl.BlockSpec(memory_space=pl.ANY)
    smem = pl.BlockSpec(memory_space=pltpu.SMEM)
    vm = pl.BlockSpec(memory_space=pltpu.VMEM)
    tokens, d_in = inputs.shape
    d_out = out_grads.shape[1]
    width = K_IN * K_OUT
    gat, gid = pl.pallas_call(
        functools.partial(project_gather_kernel, n),
        out_shape=(
            jax.ShapeDtypeStruct((n, K_IN, K_OUT), jnp.bfloat16),
            jax.ShapeDtypeStruct((n, 1, LANES), jnp.int32),
        ),
        in_specs=[smem, smem, smem, any_space, any_space],
        out_specs=(vm, vm),
        scratch_shapes=[
            vmem((HASH_ROWS, LANES)),
            vmem(((d_in // LANES + 1) * (K_IN + PAD), LANES)),
            vmem(((d_out // LANES + 1) * (K_OUT + PAD), LANES)),
            vmem((tokens, d_in), jnp.bfloat16),
            vmem((tokens, d_out), jnp.bfloat16),
            pltpu.SemaphoreType.DMA,
            pltpu.SemaphoreType.DMA,
            pltpu.SemaphoreType.DMA((n,)),
            pltpu.SemaphoreType.DMA((n,)),
            pltpu.SemaphoreType.DMA((n,)),
            pltpu.SemaphoreType.DMA((n,)),
        ],
        compiler_params=pltpu.CompilerParams(
            collective_id=0, has_side_effects=True, vmem_limit_bytes=60 << 20
        ),
    )(proj_seeds, lengths, example_ids, inputs, out_grads)
    return pl.pallas_call(
        functools.partial(finish_kernel, n),
        out_shape=(
            jax.ShapeDtypeStruct((width // n, width), jnp.float32),
            jax.ShapeDtypeStruct((1, width), jnp.float32),
            jax.ShapeDtypeStruct((1, n), jnp.float32),
        ),
        in_specs=[any_space, any_space],
        out_specs=(any_space, vm, vm),
        scratch_shapes=[
            vmem((n, K_IN, K_OUT), jnp.bfloat16),
            vmem((n, 1, LANES), jnp.int32),
            vmem(((n + 1) * K_IN, K_OUT)),
            vmem((n, width), jnp.bfloat16),
            vmem((max(width // n, K_OUT), n), jnp.bfloat16),
            vmem((n, width)),
            vmem((width // n, width)),
            pltpu.SemaphoreType.DMA((width // CHUNK,)),
            pltpu.SemaphoreType.DMA((2,)),
        ],
        compiler_params=pltpu.CompilerParams(vmem_limit_bytes=60 << 20),
    )(gat, gid)


def solution(mesh):
    rows = P(("parts", "param"), None)
    flat = P(("parts", "param"))
    return jax.shard_map(
        functools.partial(local, mesh.shape["param"]),
        mesh=mesh,
        in_specs=(rows, rows, flat, flat, P("parts")),
        out_specs=(rows, rows, rows),
        check_vma=False,
    )
```
